32 devices in a mesh: dp: 8 (over z, y), expert: 4 (over x, core).
Axes of the slice: x: 2, y: 2, z: 4, core: 2. Of those that a mesh axis runs over, the one named last changes fastest.
Arguments:
- tokens: bfloat16 [4096, 2048], P(('dp', 'expert')), may hold values from -6 to 6
- choices: int32 [4096, 2], P(('dp', 'expert')), may hold values from 0 to 4, as said below
- gate_codes: int32 [4096, 2], P(('dp', 'expert')), may hold values from 16 to 255
- hot_list: int32 [8], P('dp'), may hold values from 0 to 3
- w_in: bfloat16 [4, 2048, 1024], P('expert'), may hold values from -0.125 to 0.125
- w_down: bfloat16 [4, 512, 2048], P('expert'), may hold values from -0.25 to 0.25
Outputs:
- mixed: bfloat16 [4096, 2048], P(('dp', 'expert'))
- expert_load: float32 [4], P('expert')
The draws below stay inside these ranges and needn't reach their ends.
Inputs may be any that keep to these rules, and one draw needn't show every extreme that they name: `choices`: each row names two different values. The value 4 stands for the hot expert of the row's data group, whose own number never appears in that group's rows. The 128 rows of one device hold 4 exactly 16 times and any other value at most 80 times; on every device some value occurs exactly 80 times.
All inputs are finite; a program needn't handle non-finite values.
Results may differ from the reference program's by a relative error of at most 0.0057.
Values may be sent and summed in bfloat16 or wider, within the bound.
A program may use at most 64 MiB of HBM per device.

```python
import jax
import jax.numpy as jnp
from jax import lax

MODEL = 2048
HIDDEN_SIZE = 512
TOK_DEV = 128
TOP = 2
EXPERTS = 4
TOKENS = 4096
HOT_ROWS = 16
CAP = 80
N_DP = 8
N_EXPERT = 4


def plan_hot(key):
    return jax.random.randint(jax.random.fold_in(key, 7), (N_DP,), 0, EXPERTS).astype(jnp.int32)


def device_rows(key, hot_id):
    counter = jnp.arange(EXPERTS - 1, dtype=jnp.int32)
    others = counter + (counter >= hot_id).astype(jnp.int32)
    length = (EXPERTS - 1) * CAP
    values = jnp.repeat(others, CAP, total_repeat_length=length)
    key_list = jax.random.split(key, 4)
    chosen = others[jax.random.randint(key_list[0], (), 0, EXPERTS - 1)]
    scores = jax.random.permutation(key_list[1], length).astype(jnp.int32)
    scores = jnp.where(values == chosen, scores - length, scores)
    ranking = jnp.argsort(scores, stable=True)
    picked = jnp.sort(values[ranking[:2 * TOK_DEV - HOT_ROWS]])
    pool_ids = jnp.concatenate([jnp.full((HOT_ROWS,), EXPERTS, jnp.int32), picked])
    pair_ids = jnp.stack([pool_ids[:TOK_DEV], pool_ids[TOK_DEV:]], axis=1)
    flipped = jax.random.randint(key_list[2], (TOK_DEV, 1), 0, 2)
    pair_ids = jnp.where(flipped == 1, pair_ids[:, ::-1], pair_ids)
    return pair_ids[jax.random.permutation(key_list[3], TOK_DEV)]


def draw_choices(key, part):
    hot_ids = plan_hot(key)
    devices_all = N_DP * N_EXPERT
    dev_ids = jnp.arange(devices_all, dtype=jnp.int32)
    group_hot = hot_ids[dev_ids // N_EXPERT]
    base_key = jax.random.fold_in(key, 13)
    dev_keys = jax.vmap(lambda index: jax.random.fold_in(base_key, index))(dev_ids)
    blocks = jax.vmap(device_rows)(dev_keys, group_hot)
    return blocks.reshape(devices_all * TOK_DEV, 2).astype(jnp.int32)


def draw_hot_list(key, part):
    return plan_hot(key)


def place_ends(entries, stream_key, smallest, largest):
    longest = entries.shape.index(max(entries.shape))
    spots = []
    for shift in (0, 1):
        where = [jax.random.randint(jax.random.fold_in(stream_key, axis), (), 0, length) for axis, length in enumerate(entries.shape)]
        where[longest] = (where[longest] + shift) % entries.shape[longest]
        spots.append(tuple(where))
    return entries.at[spots[0]].set(smallest).at[spots[1]].set(largest)


def block_levels(stream_key, shape, shards, least, largest):
    level, own = 1.0, jax.random.fold_in(stream_key, 6)
    for dim, shards_of in shards:
        steps = jnp.exp(jax.random.uniform(jax.random.fold_in(own, dim), (shards_of,), jnp.float32, least / len(shards), largest / len(shards)))
        level = level * jnp.repeat(steps, shape[dim] // shards_of).reshape([-1 if axis == dim else 1 for axis in range(len(shape))])
    return level


def centred(own_key, extent, scale, limit, cuts=(), kind=jnp.bfloat16):
    factor_of = block_levels(own_key, extent, cuts, -0.22, 0.18) if cuts else 1.0
    values = jax.random.normal(own_key, extent, jnp.float32) * scale * factor_of
    return jnp.minimum(jnp.maximum(values, -limit), limit).astype(kind)


def setup_inputs(seed: int = 0) -> dict:
    seeds = jax.random.split(jax.random.key(seed), 7)
    tokens = centred(seeds[0], (TOKENS, MODEL), 1.0, 6.0, ((0, 32),))
    choices = draw_choices(jax.random.fold_in(seeds[6], 71), 0)
    gate_codes = place_ends(jax.random.randint(seeds[2], (TOKENS, TOP), 16, 256), jax.random.fold_in(seeds[2], 1), 16, 255).astype(jnp.int32)
    hot_list = draw_hot_list(jax.random.fold_in(seeds[6], 71), 0)
    w_in = centred(seeds[4], (EXPERTS, MODEL, 2 * HIDDEN_SIZE), MODEL ** -0.5, 0.125, ((0, 4),))
    w_down = centred(seeds[5], (EXPERTS, HIDDEN_SIZE, MODEL), HIDDEN_SIZE ** -0.5, 0.25, ((0, 4),))
    return {"tokens": tokens, "choices": choices, "gate_codes": gate_codes, "hot_list": hot_list, "w_in": w_in, "w_down": w_down}


def reference(tokens, choices, gate_codes, hot_list, w_in, w_down):
    tok_count = tokens.shape[0]
    group = jnp.arange(tok_count, dtype=jnp.int32) // (N_EXPERT * TOK_DEV)
    hot_tok = hot_list[group]
    experts = jnp.where(choices == EXPERTS, hot_tok[:, None], choices).astype(jnp.int32)
    gate_vals = gate_codes.astype(jnp.float32) / 256.0
    flat_ids = experts.reshape(-1)
    flat_gates = gate_vals.reshape(-1)
    expert_ids = jnp.arange(EXPERTS, dtype=jnp.int32)
    counts = jnp.sum((flat_ids[:, None] == expert_ids[None, :]).astype(jnp.int32), 0).astype(jnp.int32)
    starts = (jnp.cumsum(counts) - counts).astype(jnp.int32)
    ranking = jnp.argsort(flat_ids, stable=True).astype(jnp.int32)
    per_expert = N_DP * N_EXPERT * max(CAP, HOT_ROWS)
    ranking_pad = jnp.concatenate([ranking, jnp.zeros((per_expert,), jnp.int32)])

    def add_expert(expert_idx, combined):
        row_ids = lax.dynamic_slice_in_dim(ranking_pad, starts[expert_idx], per_expert)
        valid = jnp.arange(per_expert, dtype=jnp.int32) < counts[expert_idx]
        tok_ids = row_ids // 2
        gathered = tokens[tok_ids]
        projected = jnp.dot(gathered, w_in[expert_idx], preferred_element_type=jnp.float32)
        hidden = (jax.nn.silu(projected[:, :HIDDEN_SIZE]) * projected[:, HIDDEN_SIZE:]).astype(jnp.bfloat16)
        expert_out = jnp.dot(hidden, w_down[expert_idx], preferred_element_type=jnp.float32).astype(jnp.bfloat16)
        weight = jnp.where(valid, flat_gates[row_ids], 0.0)
        return combined.at[tok_ids].add(weight[:, None] * expert_out.astype(jnp.float32))

    combined = lax.fori_loop(0, EXPERTS, add_expert, jnp.zeros((tok_count, MODEL), jnp.float32))
    expert_load = counts.astype(jnp.float32) / (2.0 * TOK_DEV * N_DP)
    return combined.astype(jnp.bfloat16), expert_load
```

```python
import functools

import jax
import jax.numpy as jnp
from jax import lax
from jax.experimental import pallas as pl
from jax.experimental.pallas import tpu as pltpu
from jax.sharding import PartitionSpec as P

MESH = pl.DeviceIdType.MESH
CHUNKS = 4


def moe_kernel(
    n, ndp, hot_ref, choices_ref, codes_ref, tokens_ref, w_in_ref, w_down_ref,
    out_ref, load_ref,
    xbuf, pbuf, rbuf, wbuf, wcol, hid, yown, acc, win, wdown, csend, crecv,
    load_sem, x_sem, xs_send, xs_recv, xf_send, xf_recv, ws_send, ws_recv,
    wf_send, wf_recv, p_send, p_recv, r_send, r_recv, c_send, c_recv,
):
    chips = n // 2
    rows, width = tokens_ref.shape
    part = rows // CHUNKS
    hidden_width = wdown.shape[0]
    dp, me = lax.axis_index("dp"), lax.axis_index("expert")
    chip, core = me // 2, me % 2
    sibling = (dp, chip * 2 + 1 - core)

    def away(d):
        return (dp, ((chip + d) % chips) * 2 + core)

    def back(d):
        return (dp, ((chip + chips - d) % chips) * 2 + core)

    dp_steps = []
    bit = 1
    while bit < ndp:
        dp_steps.append((dp + bit - 2 * bit * ((dp // bit) % 2), me))
        bit *= 2

    barrier = pltpu.get_barrier_semaphore()
    peers = [sibling] + [away(d) for d in range(1, chips)] + dp_steps
    for peer in peers:
        pl.semaphore_signal(barrier, inc=1, device_id=peer, device_id_type=MESH)

    fetch_in = pltpu.make_async_copy(w_in_ref.at[0], win, load_sem.at[0])
    fetch_down = pltpu.make_async_copy(w_down_ref.at[0], wdown, load_sem.at[1])

    def own_rows(c):
        return pltpu.make_async_copy(
            tokens_ref.at[pl.ds(c * part, part)], xbuf.at[0, c, 0], x_sem.at[c]
        )

    for c in range(CHUNKS):
        own_rows(c).start()
    fetch_in.start()
    fetch_down.start()

    choices = choices_ref[...]
    experts = jnp.where(choices == n, hot_ref[0], choices)
    gates = codes_ref[...].astype(jnp.float32) / 256.0
    padded = wbuf.shape[2]
    ids = lax.broadcasted_iota(jnp.int32, (padded, rows), 0)
    first, second = ids == experts[0:1], ids == experts[1:2]
    wbuf[0, 0] = jnp.where(first, gates[0:1], 0.0) + jnp.where(second, gates[1:2], 0.0)
    counts = jnp.sum(first.astype(jnp.float32) + second.astype(jnp.float32), 1, keepdims=True)
    csend[0] = jnp.broadcast_to(counts, csend.shape[1:])

    pl.semaphore_wait(barrier, len(peers))

    def remote(src, dst, send, recv, device):
        return pltpu.make_async_remote_copy(
            src_ref=src, dst_ref=dst, send_sem=send, recv_sem=recv,
            device_id=device, device_id_type=MESH,
        )

    def send_weights(d):
        return remote(wbuf.at[0, 0], wbuf.at[d, 0], ws_send.at[d], ws_recv.at[d], away(d))

    def pass_weights(d):
        return remote(wbuf.at[d, 0], wbuf.at[d, 1], wf_send.at[d], wf_recv.at[d], sibling)

    def send_rows(d, c):
        return remote(
            tokens_ref.at[pl.ds(c * part, part)], xbuf.at[d, c, 0],
            xs_send.at[d, c], xs_recv.at[d, c], away(d),
        )

    def pass_rows(d, c):
        return remote(
            xbuf.at[d, c, 0], xbuf.at[d, c, 1], xf_send.at[d, c], xf_recv.at[d, c], sibling
        )

    def own_pass(c):
        return remote(
            tokens_ref.at[pl.ds(c * part, part)], xbuf.at[0, c, 1],
            xf_send.at[0, c], xf_recv.at[0, c], sibling,
        )

    def send_partial(d, c):
        return remote(
            xbuf.at[d, c, 1], pbuf.at[d, c], p_send.at[d, c], p_recv.at[d, c], sibling
        )

    def send_result(d, c):
        return remote(
            xbuf.at[d, c, 0], rbuf.at[d, c], r_send.at[d, c], r_recv.at[d, c], back(d)
        )

    def send_counts(step, device):
        src = min(step, len(dp_steps) + 1)
        return remote(
            csend.at[src], crecv.at[step], c_send.at[step], c_recv.at[step], device
        )

    for d in range(1, chips):
        send_weights(d).start()
    pass_weights(0).start()
    for c in range(CHUNKS):
        for d in range(1, chips):
            send_rows(d, c).start()
    for c in range(CHUNKS):
        own_pass(c).start()

    count_steps = dp_steps + [sibling]
    send_counts(0, count_steps[0]).start()

    def column(d, j):
        row = wbuf[d, j, pl.ds(me, 1), :]
        wide = jnp.transpose(jnp.broadcast_to(row, (rows, rows)))
        for c in range(CHUNKS):
            wcol[d, c, j] = wide[c * part : (c + 1) * part]

    def hidden_of(block, total):
        step = min(256, hidden_width)

        @pl.loop(0, hidden_width // step)
        def _(t):
            at = pl.ds(pl.multiple_of(t * step, step), step)
            at_up = pl.ds(pl.multiple_of(hidden_width + t * step, step), step)
            x = block()
            gate = jnp.dot(x, win[:, at], preferred_element_type=jnp.float32)
            up = jnp.dot(x, win[:, at_up], preferred_element_type=jnp.float32)
            hid[0:total, at] = (jax.nn.silu(gate) * up).astype(jnp.bfloat16)

    def down_of(total, weight, store):
        step = min(256, width)

        @pl.loop(0, width // step)
        def _(t):
            at = pl.ds(pl.multiple_of(t * step, step), step)
            done = jnp.dot(hid[0:total], wdown[:, at], preferred_element_type=jnp.float32)
            done = done.astype(jnp.bfloat16).astype(jnp.float32)
            store(at, done * weight()[:, 0:1])

    column(0, 0)
    pass_weights(0).wait_recv()
    column(0, 1)
    for c in range(CHUNKS):
        own_rows(c).wait()
        own_pass(c).wait_recv()
    fetch_in.wait()
    hidden_of(lambda: xbuf[0].reshape(2 * rows, width), 2 * rows)
    fetch_down.wait()

    def store_own(at, y):
        y = y.reshape(CHUNKS, 2, part, y.shape[1])
        acc[:, :, at] = y[:, 0]
        for c in range(CHUNKS):
            xbuf[0, c, 1, :, at] = y[c, 1].astype(jnp.bfloat16)

    down_of(2 * rows, lambda: wcol[0].reshape(2 * rows, rows), store_own)
    for c in range(CHUNKS):
        send_partial(0, c).start()

    def share_counts(step):
        copy = send_counts(step, count_steps[step])
        copy.wait()
        csend[step + 1] = csend[step] + crecv[step]

    for step in range(len(count_steps)):
        share_counts(step)
        if step + 1 < len(count_steps):
            send_counts(step + 1, count_steps[step + 1]).start()
    chip_steps = [(len(count_steps) + d - 1, away(d)) for d in range(1, chips)]
    for step, device in chip_steps:
        send_counts(step, device).start()

    @pl.loop(1, chips)
    def _(d):
        send_weights(d).wait_recv()
        pass_weights(d).start()
        column(d, 0)
        pass_weights(d).wait_recv()
        column(d, 1)

    @pl.loop(0, CHUNKS * (chips - 1))
    def _(item):
        c, d = item // (chips - 1), 1 + item % (chips - 1)
        send_rows(d, c).wait_recv()
        pass_rows(d, c).start()
        pass_rows(d, c).wait_recv()
        hidden_of(lambda: xbuf[d, c].reshape(2 * part, width), 2 * part)

        def store(at, y):
            yown[:, at] = y[0:part]
            xbuf[d, c, 1, :, at] = y[part:].astype(jnp.bfloat16)

        down_of(2 * part, lambda: wcol[d, c].reshape(2 * part, rows), store)
        send_partial(d, c).start()
        pass_rows(d, c).wait_send()
        send_partial(d, c).wait_recv()
        xbuf[d, c, 0] = (yown[...] + pbuf[d, c].astype(jnp.float32)).astype(jnp.bfloat16)
        send_result(d, c).start()

    total = csend[len(count_steps)]
    for step, device in chip_steps:
        send_counts(step, device).wait()
        total = total + crecv[step]
    csend[len(count_steps)] = total
    load_ref[...] = csend[len(count_steps), pl.ds(me, 1), 0:1] / (2.0 * rows * ndp)

    for c in range(CHUNKS):
        send_partial(0, c).wait_recv()
        acc[c] = acc[c] + pbuf[0, c].astype(jnp.float32)
    for c in range(CHUNKS):

        @pl.loop(1, chips)
        def _(d):
            send_result(d, c).wait_recv()
            acc[c] = acc[c] + rbuf[d, c].astype(jnp.float32)

        out_ref[c * part : (c + 1) * part, :] = acc[c].astype(jnp.bfloat16)

    pass_weights(0).wait_send()
    for c in range(CHUNKS):
        own_pass(c).wait_send()
        send_partial(0, c).wait_send()

    @pl.loop(1, chips)
    def _(d):
        send_weights(d).wait_send()
        pass_weights(d).wait_send()
        for c in range(CHUNKS):
            send_rows(d, c).wait_send()
            send_partial(d, c).wait_send()
            send_result(d, c).wait_send()


def per_device(tokens, choices, gate_codes, hot_list, w_in, w_down):
    n, ndp = lax.axis_size("expert"), lax.axis_size("dp")
    rows, width = tokens.shape
    hidden_width = w_down.shape[1]
    chips, part = n // 2, rows // CHUNKS
    padded = -(-n // 8) * 8
    steps = (ndp - 1).bit_length() + 1
    bf16, f32 = jnp.bfloat16, jnp.float32
    dma = pltpu.SemaphoreType.DMA
    vmem = pl.BlockSpec(memory_space=pltpu.VMEM)
    mixed, load = pl.pallas_call(
        functools.partial(moe_kernel, n, ndp),
        out_shape=(
            jax.ShapeDtypeStruct((rows, width), bf16),
            jax.ShapeDtypeStruct((1, 1), f32),
        ),
        in_specs=[pl.BlockSpec(memory_space=pltpu.SMEM), vmem, vmem]
        + [pl.BlockSpec(memory_space=pl.ANY)] * 3,
        out_specs=(vmem, vmem),
        scratch_shapes=[
            pltpu.VMEM((chips, CHUNKS, 2, part, width), bf16),
            pltpu.VMEM((chips, CHUNKS, part, width), bf16),
            pltpu.VMEM((chips, CHUNKS, part, width), bf16),
            pltpu.VMEM((chips, 2, padded, rows), f32),
            pltpu.VMEM((chips, CHUNKS, 2, part, rows), f32),
            pltpu.VMEM((2 * rows, hidden_width), bf16),
            pltpu.VMEM((part, width), f32),
            pltpu.VMEM((CHUNKS, part, width), f32),
            pltpu.VMEM(w_in.shape[1:], bf16),
            pltpu.VMEM(w_down.shape[1:], bf16),
            pltpu.VMEM((steps + 1, padded, 128), f32),
            pltpu.VMEM((steps + chips - 1, padded, 128), f32),
            dma((2,)), dma((CHUNKS,)),
            dma((chips, CHUNKS)), dma((chips, CHUNKS)),
            dma((chips, CHUNKS)), dma((chips, CHUNKS)),
            dma((chips,)), dma((chips,)),
            dma((chips,)), dma((chips,)),
            dma((chips, CHUNKS)), dma((chips, CHUNKS)),
            dma((chips, CHUNKS)), dma((chips, CHUNKS)),
            dma((steps + chips - 1,)), dma((steps + chips - 1,)),
        ],
        compiler_params=pltpu.CompilerParams(
            collective_id=0, has_side_effects=True, vmem_limit_bytes=58 * 2**20
        ),
    )(hot_list, choices.T, gate_codes.T, tokens, w_in, w_down)
    return mixed, load.reshape(1)


def solution(mesh):
    return jax.shard_map(
        per_device,
        mesh=mesh,
        in_specs=(
            P(("dp", "expert"), None),
            P(("dp", "expert"), None),
            P(("dp", "expert"), None),
            P("dp"),
            P("expert", None, None),
            P("expert", None, None),
        ),
        out_specs=(P(("dp", "expert"), None), P("expert")),
        check_vma=False,
    )
```

```python
import functools

import jax
import jax.numpy as jnp
from jax import lax
from jax.experimental import pallas as pl
from jax.experimental.pallas import tpu as pltpu
from jax.sharding import PartitionSpec as P

MESH = pl.DeviceIdType.MESH
CHUNKS = 4


def moe_kernel(
    n, ndp, hot_ref, choices_ref, codes_ref, tokens_ref, w_in_ref, w_down_ref,
    out_ref, load_ref,
    xbuf, pbuf, rbuf, wbuf, wcol, hid, yown, acc, win, wdown, csend, crecv,
    load_sem, x_sem, xs_send, xs_recv, xf_send, xf_recv, ws_send, ws_recv,
    wf_send, wf_recv, p_send, p_recv, r_send, r_recv, c_send, c_recv,
):
    chips = n // 2
    rows, width = tokens_ref.shape
    part = rows // CHUNKS
    hidden_width = wdown.shape[0]
    dp, me = lax.axis_index("dp"), lax.axis_index("expert")
    chip, core = me // 2, me % 2
    sibling = (dp, chip * 2 + 1 - core)

    def away(d):
        return (dp, ((chip + d) % chips) * 2 + core)

    def back(d):
        return (dp, ((chip + chips - d) % chips) * 2 + core)

    dp_steps = []
    bit = 1
    while bit < ndp:
        dp_steps.append((dp + bit - 2 * bit * ((dp // bit) % 2), me))
        bit *= 2

    barrier = pltpu.get_barrier_semaphore()
    peers = [sibling] + [away(d) for d in range(1, chips)] + dp_steps
    for peer in peers:
        pl.semaphore_signal(barrier, inc=1, device_id=peer, device_id_type=MESH)

    fetch_in = pltpu.make_async_copy(w_in_ref.at[0], win, load_sem.at[0])
    fetch_down = pltpu.make_async_copy(w_down_ref.at[0], wdown, load_sem.at[1])

    def own_rows(c):
        return pltpu.make_async_copy(
            tokens_ref.at[pl.ds(c * part, part)], xbuf.at[0, c, 0], x_sem.at[c]
        )

    for c in range(CHUNKS):
        own_rows(c).start()
    fetch_in.start()
    fetch_down.start()

    choices = choices_ref[...]
    experts = jnp.where(choices == n, hot_ref[0], choices)
    gates = codes_ref[...].astype(jnp.float32) / 256.0
    padded = wbuf.shape[2]
    ids = lax.broadcasted_iota(jnp.int32, (padded, rows), 0)
    first, second = ids == experts[0:1], ids == experts[1:2]
    wbuf[0, 0] = jnp.where(first, gates[0:1], 0.0) + jnp.where(second, gates[1:2], 0.0)
    counts = jnp.sum(first.astype(jnp.float32) + second.astype(jnp.float32), 1, keepdims=True)
    csend[0] = jnp.broadcast_to(counts, csend.shape[1:])

    pl.semaphore_wait(barrier, len(peers))

    def remote(src, dst, send, recv, device):
        return pltpu.make_async_remote_copy(
            src_ref=src, dst_ref=dst, send_sem=send, recv_sem=recv,
            device_id=device, device_id_type=MESH,
        )

    def send_weights(d):
        return remote(wbuf.at[0, 0], wbuf.at[d, 0], ws_send.at[d], ws_recv.at[d], away(d))

    def pass_weights(d):
        return remote(wbuf.at[d, 0], wbuf.at[d, 1], wf_send.at[d], wf_recv.at[d], sibling)

    def send_rows(d, c):
        return remote(
            tokens_ref.at[pl.ds(c * part, part)], xbuf.at[d, c, 0],
            xs_send.at[d, c], xs_recv.at[d, c], away(d),
        )

    def pass_rows(d, c):
        return remote(
            xbuf.at[d, c, 0], xbuf.at[d, c, 1], xf_send.at[d, c], xf_recv.at[d, c], sibling
        )

    def own_pass(c):
        return remote(
            tokens_ref.at[pl.ds(c * part, part)], xbuf.at[0, c, 1],
            xf_send.at[0, c], xf_recv.at[0, c], sibling,
        )

    def send_partial(d, c):
        return remote(
            xbuf.at[d, c, 1], pbuf.at[d, c], p_send.at[d, c], p_recv.at[d, c], sibling
        )

    def send_result(d, c):
        return remote(
            xbuf.at[d, c, 0], rbuf.at[d, c], r_send.at[d, c], r_recv.at[d, c], back(d)
        )

    def send_counts(step, device):
        src = min(step, len(dp_steps) + 1)
        return remote(
            csend.at[src], crecv.at[step], c_send.at[step], c_recv.at[step], device
        )

    for d in range(1, chips):
        send_weights(d).start()
    pass_weights(0).start()
    for c in range(CHUNKS):
        for d in range(1, chips):
            send_rows(d, c).start()
    for c in range(CHUNKS):
        own_pass(c).start()

    count_steps = dp_steps + [sibling]
    send_counts(0, count_steps[0]).start()

    chip_steps = [(len(count_steps) + d - 1, away(d)) for d in range(1, chips)]

    def share_counts(step):
        send_counts(step, count_steps[step]).wait()
        csend[step + 1] = csend[step] + crecv[step]
        if step + 1 < len(count_steps):
            send_counts(step + 1, count_steps[step + 1]).start()
        else:
            for later, device in chip_steps:
                send_counts(later, device).start()

    def column(d, j):
        row = wbuf[d, j, pl.ds(me, 1), :]
        wide = jnp.transpose(jnp.broadcast_to(row, (rows, rows)))
        for c in range(CHUNKS):
            wcol[d, c, j] = wide[c * part : (c + 1) * part]

    def hidden_of(block, total):
        step = min(256, hidden_width)

        @pl.loop(0, hidden_width // step, unroll=True)
        def _(t):
            at = pl.ds(pl.multiple_of(t * step, step), step)
            at_up = pl.ds(pl.multiple_of(hidden_width + t * step, step), step)
            x = block()
            gate = jnp.dot(x, win[:, at], preferred_element_type=jnp.float32)
            up = jnp.dot(x, win[:, at_up], preferred_element_type=jnp.float32)
            hid[0:total, at] = (jax.nn.silu(gate) * up).astype(jnp.bfloat16)

    def down_of(total, weight, store):
        step = min(256, width)

        @pl.loop(0, width // step, unroll=True)
        def _(t):
            at = pl.ds(pl.multiple_of(t * step, step), step)
            done = jnp.dot(hid[0:total], wdown[:, at], preferred_element_type=jnp.float32)
            done = done.astype(jnp.bfloat16).astype(jnp.float32)
            store(at, done * weight()[:, 0:1])

    column(0, 0)
    pass_weights(0).wait_recv()
    column(0, 1)
    for c in range(CHUNKS):
        own_rows(c).wait()
        own_pass(c).wait_recv()
    fetch_in.wait()
    hidden_of(lambda: xbuf[0].reshape(2 * rows, width), 2 * rows)
    share_counts(0)
    fetch_down.wait()

    def store_own(at, y):
        y = y.reshape(CHUNKS, 2, part, y.shape[1])
        acc[:, :, at] = y[:, 0]
        for c in range(CHUNKS):
            xbuf[0, c, 1, :, at] = y[c, 1].astype(jnp.bfloat16)

    down_of(2 * rows, lambda: wcol[0].reshape(2 * rows, rows), store_own)
    for c in range(CHUNKS):
        send_partial(0, c).start()
    for step in range(1, min(2, len(count_steps))):
        share_counts(step)

    @pl.loop(1, chips)
    def _(d):
        send_weights(d).wait_recv()
        pass_weights(d).start()
        column(d, 0)
        pass_weights(d).wait_recv()
        column(d, 1)

    items = CHUNKS * (chips - 1)

    def place(item):
        return 1 + item % (chips - 1), item // (chips - 1)

    def hand_over(item):
        d, c = place(item)
        send_rows(d, c).wait_recv()
        pass_rows(d, c).start()

    hand_over(0)

    @pl.loop(0, items)
    def _(item):
        d, c = place(item)
        pass_rows(d, c).wait_recv()
        hidden_of(lambda: xbuf[d, c].reshape(2 * part, width), 2 * part)

        def store(at, y):
            yown[:, at] = y[0:part]
            xbuf[d, c, 1, :, at] = y[part:].astype(jnp.bfloat16)

        down_of(2 * part, lambda: wcol[d, c].reshape(2 * part, rows), store)
        send_partial(d, c).start()

        @pl.when(item + 1 < items)
        def _():
            hand_over(item + 1)

        pass_rows(d, c).wait_send()
        send_partial(d, c).wait_recv()
        xbuf[d, c, 0] = (yown[...] + pbuf[d, c].astype(jnp.float32)).astype(jnp.bfloat16)
        send_result(d, c).start()

    for c in range(CHUNKS):
        send_partial(0, c).wait_recv()
        acc[c] = acc[c] + pbuf[0, c].astype(jnp.float32)
    for step in range(min(2, len(count_steps)), len(count_steps)):
        share_counts(step)
    total = csend[len(count_steps)]
    for step, device in chip_steps:
        send_counts(step, device).wait()
        total = total + crecv[step]
    csend[len(count_steps)] = total
    load_ref[...] = csend[len(count_steps), pl.ds(me, 1), 0:1] / (2.0 * rows * ndp)

    for c in range(CHUNKS):

        @pl.loop(1, chips)
        def _(d):
            send_result(d, c).wait_recv()
            acc[c] = acc[c] + rbuf[d, c].astype(jnp.float32)

        out_ref[c * part : (c + 1) * part, :] = acc[c].astype(jnp.bfloat16)

    pass_weights(0).wait_send()
    for c in range(CHUNKS):
        own_pass(c).wait_send()
        send_partial(0, c).wait_send()

    @pl.loop(1, chips)
    def _(d):
        send_weights(d).wait_send()
        pass_weights(d).wait_send()
        for c in range(CHUNKS):
            send_rows(d, c).wait_send()
            send_partial(d, c).wait_send()
            send_result(d, c).wait_send()


def per_device(tokens, choices, gate_codes, hot_list, w_in, w_down):
    n, ndp = lax.axis_size("expert"), lax.axis_size("dp")
    rows, width = tokens.shape
    hidden_width = w_down.shape[1]
    chips, part = n // 2, rows // CHUNKS
    padded = -(-n // 8) * 8
    steps = (ndp - 1).bit_length() + 1
    bf16, f32 = jnp.bfloat16, jnp.float32
    dma = pltpu.SemaphoreType.DMA
    vmem = pl.BlockSpec(memory_space=pltpu.VMEM)
    mixed, load = pl.pallas_call(
        functools.partial(moe_kernel, n, ndp),
        out_shape=(
            jax.ShapeDtypeStruct((rows, width), bf16),
            jax.ShapeDtypeStruct((1, 1), f32),
        ),
        in_specs=[pl.BlockSpec(memory_space=pltpu.SMEM), vmem, vmem]
        + [pl.BlockSpec(memory_space=pl.ANY)] * 3,
        out_specs=(vmem, vmem),
        scratch_shapes=[
            pltpu.VMEM((chips, CHUNKS, 2, part, width), bf16),
            pltpu.VMEM((chips, CHUNKS, part, width), bf16),
            pltpu.VMEM((chips, CHUNKS, part, width), bf16),
            pltpu.VMEM((chips, 2, padded, rows), f32),
            pltpu.VMEM((chips, CHUNKS, 2, part, rows), f32),
            pltpu.VMEM((2 * rows, hidden_width), bf16),
            pltpu.VMEM((part, width), f32),
            pltpu.VMEM((CHUNKS, part, width), f32),
            pltpu.VMEM(w_in.shape[1:], bf16),
            pltpu.VMEM(w_down.shape[1:], bf16),
            pltpu.VMEM((steps + 1, padded, 128), f32),
            pltpu.VMEM((steps + chips - 1, padded, 128), f32),
            dma((2,)), dma((CHUNKS,)),
            dma((chips, CHUNKS)), dma((chips, CHUNKS)),
            dma((chips, CHUNKS)), dma((chips, CHUNKS)),
            dma((chips,)), dma((chips,)),
            dma((chips,)), dma((chips,)),
            dma((chips, CHUNKS)), dma((chips, CHUNKS)),
            dma((chips, CHUNKS)), dma((chips, CHUNKS)),
            dma((steps + chips - 1,)), dma((steps + chips - 1,)),
        ],
        compiler_params=pltpu.CompilerParams(
            collective_id=0, has_side_effects=True, vmem_limit_bytes=58 * 2**20
        ),
    )(hot_list, choices.T, gate_codes.T, tokens, w_in, w_down)
    return mixed, load.reshape(1)


def solution(mesh):
    return jax.shard_map(
        per_device,
        mesh=mesh,
        in_specs=(
            P(("dp", "expert"), None),
            P(("dp", "expert"), None),
            P(("dp", "expert"), None),
            P("dp"),
            P("expert", None, None),
            P("expert", None, None),
        ),
        out_specs=(P(("dp", "expert"), None), P("expert")),
        check_vma=False,
    )
```

```python
import functools

import jax
import jax.numpy as jnp
from jax import lax
from jax.experimental import pallas as pl
from jax.experimental.pallas import tpu as pltpu
from jax.sharding import PartitionSpec as P

MESH = pl.DeviceIdType.MESH
CHUNKS = 4


def moe_kernel(
    n, ndp, hot_ref, choices_ref, codes_ref, tokens_ref, w_in_ref, w_down_ref,
    out_ref, load_ref,
    xbuf, pbuf, rbuf, wbuf, wcol, hid, yown, acc, win, wdown, csend, crecv,
    load_sem, x_sem, xs_send, xs_recv, xf_send, xf_recv, ws_send, ws_recv,
    wf_send, wf_recv, p_send, p_recv, r_send, r_recv, c_send, c_recv,
):
    chips = n // 2
    rows, width = tokens_ref.shape
    part = rows // CHUNKS
    hidden_width = wdown.shape[0]
    dp, me = lax.axis_index("dp"), lax.axis_index("expert")
    chip, core = me // 2, me % 2
    sibling = (dp, chip * 2 + 1 - core)

    def away(d):
        return (dp, ((chip + d) % chips) * 2 + core)

    def back(d):
        return (dp, ((chip + chips - d) % chips) * 2 + core)

    dp_steps = []
    bit = 1
    while bit < ndp:
        dp_steps.append((dp + bit - 2 * bit * ((dp // bit) % 2), me))
        bit *= 2

    barrier = pltpu.get_barrier_semaphore()
    peers = [sibling] + [away(d) for d in range(1, chips)] + dp_steps
    for peer in peers:
        pl.semaphore_signal(barrier, inc=1, device_id=peer, device_id_type=MESH)

    fetch_in = pltpu.make_async_copy(w_in_ref.at[0], win, load_sem.at[0])
    fetch_down = pltpu.make_async_copy(w_down_ref.at[0], wdown, load_sem.at[1])

    def own_rows(c):
        return pltpu.make_async_copy(
            tokens_ref.at[pl.ds(c * part, part)], xbuf.at[0, c, 0], x_sem.at[c]
        )

    for c in range(CHUNKS):
        own_rows(c).start()
    fetch_in.start()
    fetch_down.start()

    choices = choices_ref[...]
    experts = jnp.where(choices == n, hot_ref[0], choices)
    gates = codes_ref[...].astype(jnp.float32) / 256.0
    padded = wbuf.shape[2]
    ids = lax.broadcasted_iota(jnp.int32, (padded, rows), 0)
    first, second = ids == experts[0:1], ids == experts[1:2]
    wbuf[0, 0] = jnp.where(first, gates[0:1], 0.0) + jnp.where(second, gates[1:2], 0.0)
    counts = jnp.sum(first.astype(jnp.float32) + second.astype(jnp.float32), 1, keepdims=True)
    csend[0] = jnp.broadcast_to(counts, csend.shape[1:])

    for c in range(CHUNKS):
        own_rows(c).wait()
    pl.semaphore_wait(barrier, len(peers))

    def remote(src, dst, send, recv, device):
        return pltpu.make_async_remote_copy(
            src_ref=src, dst_ref=dst, send_sem=send, recv_sem=recv,
            device_id=device, device_id_type=MESH,
        )

    def send_weights(d):
        return remote(wbuf.at[0, 0], wbuf.at[d, 0], ws_send.at[d], ws_recv.at[d], away(d))

    def pass_weights(d):
        return remote(wbuf.at[d, 0], wbuf.at[d, 1], wf_send.at[d], wf_recv.at[d], sibling)

    def send_rows(d, c):
        return remote(
            xbuf.at[0, c, 0], xbuf.at[d, c, 0],
            xs_send.at[d, c], xs_recv.at[d, c], away(d),
        )

    def pass_rows(d, c):
        return remote(
            xbuf.at[d, c, 0], xbuf.at[d, c, 1], xf_send.at[d, c], xf_recv.at[d, c], sibling
        )

    def own_pass(c):
        return remote(
            xbuf.at[0, c, 0], xbuf.at[0, c, 1],
            xf_send.at[0, c], xf_recv.at[0, c], sibling,
        )

    def send_partial(d, c):
        return remote(
            xbuf.at[d, c, 1], pbuf.at[d, c], p_send.at[d, c], p_recv.at[d, c], sibling
        )

    def send_result(d, c):
        return remote(
            xbuf.at[d, c, 0], rbuf.at[d, c], r_send.at[d, c], r_recv.at[d, c], back(d)
        )

    def send_counts(step, device):
        src = min(step, len(dp_steps) + 1)
        return remote(
            csend.at[src], crecv.at[step], c_send.at[step], c_recv.at[step], device
        )

    count_steps = dp_steps + [sibling]
    send_counts(0, count_steps[0]).start()
    for d in range(1, chips):
        send_weights(d).start()
    pass_weights(0).start()
    for c in range(CHUNKS):
        for d in range(1, chips):
            send_rows(d, c).start()
    for c in range(CHUNKS):
        own_pass(c).start()

    chip_steps = [(len(count_steps) + d - 1, away(d)) for d in range(1, chips)]

    def share_counts(step):
        send_counts(step, count_steps[step]).wait()
        csend[step + 1] = csend[step] + crecv[step]
        if step + 1 < len(count_steps):
            send_counts(step + 1, count_steps[step + 1]).start()
        else:
            for later, device in chip_steps:
                send_counts(later, device).start()

    def column(d, j):
        row = wbuf[d, j, pl.ds(me, 1), :]
        wide = jnp.transpose(jnp.broadcast_to(row, (rows, rows)))
        for c in range(CHUNKS):
            wcol[d, c, j] = wide[c * part : (c + 1) * part]

    def hidden_of(block, total):
        step = min(256, hidden_width)

        @pl.loop(0, hidden_width // step, unroll=True)
        def _(t):
            at = pl.ds(pl.multiple_of(t * step, step), step)
            at_up = pl.ds(pl.multiple_of(hidden_width + t * step, step), step)
            x = block()
            gate = jnp.dot(x, win[:, at], preferred_element_type=jnp.float32)
            up = jnp.dot(x, win[:, at_up], preferred_element_type=jnp.float32)
            hid[0:total, at] = (jax.nn.silu(gate) * up).astype(jnp.bfloat16)

    def down_of(total, weight, store):
        step = min(256, width)

        @pl.loop(0, width // step, unroll=True)
        def _(t):
            at = pl.ds(pl.multiple_of(t * step, step), step)
            done = jnp.dot(hid[0:total], wdown[:, at], preferred_element_type=jnp.float32)
            done = done.astype(jnp.bfloat16).astype(jnp.float32)
            store(at, done * weight()[:, 0:1])

    column(0, 0)
    pass_weights(0).wait_recv()
    column(0, 1)
    for c in range(CHUNKS):
        own_pass(c).wait_recv()
    fetch_in.wait()
    hidden_of(lambda: xbuf[0].reshape(2 * rows, width), 2 * rows)
    share_counts(0)
    fetch_down.wait()

    def store_own(at, y):
        y = y.reshape(CHUNKS, 2, part, y.shape[1])
        acc[:, :, at] = y[:, 0]
        for c in range(CHUNKS):
            xbuf[0, c, 1, :, at] = y[c, 1].astype(jnp.bfloat16)

    down_of(2 * rows, lambda: wcol[0].reshape(2 * rows, rows), store_own)
    for c in range(CHUNKS):
        send_partial(0, c).start()
    for step in range(1, min(2, len(count_steps))):
        share_counts(step)

    @pl.loop(1, chips)
    def _(d):
        send_weights(d).wait_recv()
        pass_weights(d).start()
        column(d, 0)
        pass_weights(d).wait_recv()
        column(d, 1)

    items = CHUNKS * (chips - 1)

    def place(item):
        return 1 + item % (chips - 1), item // (chips - 1)

    def hand_over(item):
        d, c = place(item)
        send_rows(d, c).wait_recv()
        pass_rows(d, c).start()

    hand_over(0)

    @pl.loop(0, items)
    def _(item):
        d, c = place(item)
        pass_rows(d, c).wait_recv()
        hidden_of(lambda: xbuf[d, c].reshape(2 * part, width), 2 * part)

        def store(at, y):
            yown[:, at] = y[0:part]
            xbuf[d, c, 1, :, at] = y[part:].astype(jnp.bfloat16)

        down_of(2 * part, lambda: wcol[d, c].reshape(2 * part, rows), store)
        send_partial(d, c).start()

        for step in range(2, min(2 + items, len(count_steps))):
            pl.when(item == step - 2)(functools.partial(share_counts, step))

        @pl.when(item + 1 < items)
        def _():
            hand_over(item + 1)

        pass_rows(d, c).wait_send()
        send_partial(d, c).wait_recv()
        xbuf[d, c, 0] = (yown[...] + pbuf[d, c].astype(jnp.float32)).astype(jnp.bfloat16)
        send_result(d, c).start()

    for c in range(CHUNKS):
        send_partial(0, c).wait_recv()
        acc[c] = acc[c] + pbuf[0, c].astype(jnp.float32)
    for step in range(2 + items, len(count_steps)):
        share_counts(step)
    total = csend[len(count_steps)]
    for step, device in chip_steps:
        send_counts(step, device).wait()
        total = total + crecv[step]
    csend[len(count_steps)] = total
    load_ref[...] = csend[len(count_steps), pl.ds(me, 1), 0:1] / (2.0 * rows * ndp)

    for c in range(CHUNKS):

        @pl.loop(1, chips)
        def _(d):
            send_result(d, c).wait_recv()
            acc[c] = acc[c] + rbuf[d, c].astype(jnp.float32)

        out_ref[c * part : (c + 1) * part, :] = acc[c].astype(jnp.bfloat16)

    pass_weights(0).wait_send()
    for c in range(CHUNKS):
        own_pass(c).wait_send()
        send_partial(0, c).wait_send()

    @pl.loop(1, chips)
    def _(d):
        send_weights(d).wait_send()
        pass_weights(d).wait_send()
        for c in range(CHUNKS):
            send_rows(d, c).wait_send()
            send_partial(d, c).wait_send()
            send_result(d, c).wait_send()


def per_device(tokens, choices, gate_codes, hot_list, w_in, w_down):
    n, ndp = lax.axis_size("expert"), lax.axis_size("dp")
    rows, width = tokens.shape
    hidden_width = w_down.shape[1]
    chips, part = n // 2, rows // CHUNKS
    padded = -(-n // 8) * 8
    steps = (ndp - 1).bit_length() + 1
    bf16, f32 = jnp.bfloat16, jnp.float32
    dma = pltpu.SemaphoreType.DMA
    vmem = pl.BlockSpec(memory_space=pltpu.VMEM)
    mixed, load = pl.pallas_call(
        functools.partial(moe_kernel, n, ndp),
        out_shape=(
            jax.ShapeDtypeStruct((rows, width), bf16),
            jax.ShapeDtypeStruct((1, 1), f32),
        ),
        in_specs=[pl.BlockSpec(memory_space=pltpu.SMEM), vmem, vmem]
        + [pl.BlockSpec(memory_space=pl.ANY)] * 3,
        out_specs=(vmem, vmem),
        scratch_shapes=[
            pltpu.VMEM((chips, CHUNKS, 2, part, width), bf16),
            pltpu.VMEM((chips, CHUNKS, part, width), bf16),
            pltpu.VMEM((chips, CHUNKS, part, width), bf16),
            pltpu.VMEM((chips, 2, padded, rows), f32),
            pltpu.VMEM((chips, CHUNKS, 2, part, rows), f32),
            pltpu.VMEM((2 * rows, hidden_width), bf16),
            pltpu.VMEM((part, width), f32),
            pltpu.VMEM((CHUNKS, part, width), f32),
            pltpu.VMEM(w_in.shape[1:], bf16),
            pltpu.VMEM(w_down.shape[1:], bf16),
            pltpu.VMEM((steps + 1, padded, 128), f32),
            pltpu.VMEM((steps + chips - 1, padded, 128), f32),
            dma((2,)), dma((CHUNKS,)),
            dma((chips, CHUNKS)), dma((chips, CHUNKS)),
            dma((chips, CHUNKS)), dma((chips, CHUNKS)),
            dma((chips,)), dma((chips,)),
            dma((chips,)), dma((chips,)),
            dma((chips, CHUNKS)), dma((chips, CHUNKS)),
            dma((chips, CHUNKS)), dma((chips, CHUNKS)),
            dma((steps + chips - 1,)), dma((steps + chips - 1,)),
        ],
        compiler_params=pltpu.CompilerParams(
            collective_id=0, has_side_effects=True, vmem_limit_bytes=58 * 2**20
        ),
    )(hot_list, choices.T, gate_codes.T, tokens, w_in, w_down)
    return mixed, load.reshape(1)


def solution(mesh):
    return jax.shard_map(
        per_device,
        mesh=mesh,
        in_specs=(
            P(("dp", "expert"), None),
            P(("dp", "expert"), None),
            P(("dp", "expert"), None),
            P("dp"),
            P("expert", None, None),
            P("expert", None, None),
        ),
        out_specs=(P(("dp", "expert"), None), P("expert")),
        check_vma=False,
    )
```
